256 devices in a mesh: grp: 32 (over x_hi, z, core), blk: 8 (over x_lo, y).
Axes of the slice: x: 4 (x_hi: 2, x_lo: 2; x = x_hi * 2 + x_lo), y: 4, z: 8, core: 2. Of those that a mesh axis runs over, the one named last changes fastest.
Arguments:
- spectra: bfloat16 [8192, 2, 4, 512], P(('grp', 'blk')), may hold values from -6 to 6
- ownership: int32 [32, 8], replicated, may hold values from 0 to 7, each once within a row
- pairing: int32 [32], replicated, may hold values from 0 to 31, as said below
Outputs:
- near_corr: bfloat16 [8192, 256, 128], P(('grp', 'blk'))
- far_corr: bfloat16 [8192, 256, 128], P(('grp', 'blk'))
The draws below stay inside these ranges and needn't reach their ends.
Inputs may be any that keep to these rules, and one draw needn't show every extreme that they name: pairing[g] = g XOR m for all g, with one m of 1 to 31 for the round; so each group is its partner's partner and never its own.
All inputs are finite; a program needn't handle non-finite values.
Results may differ from the reference program's by a relative error of at most 0.0055.
Values may be sent and summed in bfloat16 or wider, within the bound.
No kernel may reach another device: no remote copies, remote signals or barrier semaphores. Data moves between devices by JAX's collectives and lax.ppermute only.
A program may use at most 128 MiB of HBM per device.

```python
import jax
import jax.numpy as jnp
from jax import lax

F = 512
LAGS = 128
W = 4
CH_DEV = 32
CH_GRP = 256
CHANNELS = 8192
N_GRP = 32
N_BLK = 8


def draw_pairing(key, part):
    key = jax.random.fold_in(key, 7)
    offset = jax.random.randint(key, (), 1, N_GRP).astype(jnp.int32)
    return jnp.bitwise_xor(jnp.arange(N_GRP, dtype=jnp.int32), offset)


def level_of(own_key, extent, shards, least, top_value):
    level = 1.0
    for dim, blocks in shards:
        heights = jax.random.uniform(jax.random.fold_in(jax.random.fold_in(own_key, 6), dim), (blocks,), jnp.float32, least / len(shards), top_value / len(shards))
        level = level * jnp.repeat(jnp.exp(heights), extent[dim] // blocks).reshape((-1,) + (1,) * (len(extent) - 1 - dim))
    return level


def normal_values(rng, extent, scale, reach, cuts=(), kind=jnp.bfloat16):
    gain = level_of(rng, extent, cuts, -0.22, 0.18) if cuts else 1.0
    values = jax.random.normal(rng, extent, jnp.float32) * scale * gain
    return jnp.minimum(jnp.maximum(values, -reach), reach).astype(kind)


def setup_inputs(seed: int = 0) -> dict:
    arg_keys = jax.random.split(jax.random.key(seed), 4)
    return {
        "spectra": normal_values(arg_keys[0], (CHANNELS, 2, W, F), 1.0, 6.0, ((0, 256),)),
        "ownership": jax.vmap(lambda own: jax.random.permutation(own, N_BLK))(jax.random.split(arg_keys[1], N_GRP)).reshape((N_GRP, N_BLK)).astype(jnp.int32),
        "pairing": draw_pairing(jax.random.fold_in(arg_keys[3], 71), 0),
    }


def make_twiddle(freq_count, lag_count):
    freqs = jnp.arange(freq_count, dtype=jnp.int32)[:, None]
    shifts = jnp.arange(lag_count, dtype=jnp.int32)[None, :] - lag_count // 2
    phase = jnp.mod(freqs * shifts, 2 * freq_count).astype(jnp.float32)
    angle = jnp.float32(jnp.pi) * phase / jnp.float32(freq_count)
    return jnp.stack([jnp.cos(angle), -jnp.sin(angle)], 0).astype(jnp.bfloat16)

def correlate(own_rows, other_rows, twiddle):
    row_count = own_rows.shape[0]
    col_count = other_rows.shape[0]
    real_part = own_rows[:, 0].astype(jnp.float32)
    imag_part = own_rows[:, 1].astype(jnp.float32)
    first = jnp.concatenate([real_part, imag_part], 1)
    second = jnp.concatenate([imag_part, -real_part], 1)
    left_side = jnp.concatenate([first, second], 0)
    right_side = jnp.concatenate([other_rows[:, 0], other_rows[:, 1]], 1).astype(jnp.float32)
    cross = lax.dot_general(left_side, right_side, (((1,), (1,)), ((2,), (2,))), precision=lax.Precision.HIGHEST, preferred_element_type=jnp.float32)
    cross = (cross * jnp.float32(1.0 / W)).astype(jnp.bfloat16)
    cross = cross.reshape(cross.shape[0], 2, row_count, col_count).astype(jnp.float32)
    result = lax.dot_general(cross, twiddle.astype(jnp.float32), (((0, 1), (1, 0)), ((), ())), precision=lax.Precision.HIGHEST, preferred_element_type=jnp.float32)
    scale = jnp.float32(1.0) / jnp.sqrt(jnp.float32(F))
    return (result * scale).astype(jnp.bfloat16)

def reference(spectra, ownership, pairing):
    twiddle = make_twiddle(F, LAGS)
    blocked = spectra.reshape(N_GRP, N_BLK, CH_DEV, 2, W, F)
    inverse = jnp.argsort(ownership, axis=1).astype(jnp.int32)
    ordered = jnp.take_along_axis(blocked, inverse[:, :, None, None, None, None], axis=1)
    ordered = ordered.reshape(N_GRP, CH_GRP, 2, W, F)
    stored = blocked.reshape(N_GRP, CH_GRP, 2, W, F)

    def one_group(group_index):
        own_rows = stored[group_index]
        near_part = correlate(own_rows, ordered[group_index], twiddle)
        far_part = correlate(own_rows, ordered[pairing[group_index]], twiddle)
        return (near_part, far_part)
    near_corr, far_corr = lax.map(one_group, jnp.arange(N_GRP, dtype=jnp.int32))
    return (near_corr.reshape(CHANNELS, CH_GRP, LAGS), far_corr.reshape(CHANNELS, CH_GRP, LAGS))
```

```python
import functools

import jax
import jax.numpy as jnp
import ml_dtypes
import numpy as np
from jax import lax
from jax.experimental import pallas as pl
from jax.experimental.pallas import tpu as pltpu
from jax.sharding import PartitionSpec as P

LAGS = 128
ROWS = 8


def twiddle_table(freq_count, lag_count):
    freqs = np.arange(freq_count)[None, :]
    shifts = np.arange(lag_count)[:, None] - lag_count // 2
    angle = np.pi * ((freqs * shifts) % (2 * freq_count)) / freq_count
    return np.stack([np.cos(angle), -np.sin(angle)]).astype(ml_dtypes.bfloat16)


def sources(place):
    column, y = place // 4 * 4, place % 4
    up, down, over = (y + 1) % 4, (y + 3) % 4, (y + 2) % 4
    other = 4 - column
    return (
        column + y, other + y, column + down, column + up,
        column + over, other + down, other + up, other + over,
    )


def send(block, step):
    return lax.ppermute(block, "blk", [(i, step(i)) for i in range(8)])


def across(block):
    return send(block, lambda i: i ^ 4)


def upward(block):
    return send(block, lambda i: i & 4 | (i + 1) & 3)


def downward(block):
    return send(block, lambda i: i & 4 | (i - 1) & 3)


def gather(block):
    half = block.shape[0] // 2
    beside = across(block)
    below = upward(block)
    above = downward(block)
    far_side = jnp.concatenate([upward(below[:half]), downward(above[half:])], 0)
    beside_below = upward(beside)
    beside_above = downward(beside)
    beside_far = across(far_side)
    return block, beside, below, above, far_side, beside_below, beside_above, beside_far


def exchange(block, mask):
    count = lax.axis_size("grp")
    branches = [
        functools.partial(lax.ppermute, axis_name="grp", perm=[(i, i ^ m) for i in range(count)])
        for m in range(1, count)
    ]
    return lax.switch(mask - 1, branches, block)


def correlate_kernel(far, ownership, pairing, x_ref, twiddle_ref, *refs):
    blocks, (out_ref, y_ref, yt_ref, left_ref, sems) = refs[:8], refs[8:]
    step = pl.program_id(0)
    depth = y_ref.shape[1]
    lags, freqs = twiddle_ref.shape[1:]
    windows = depth // freqs // 2
    height = blocks[0].shape[0]

    @pl.when(step == 0)
    def _():
        group = lax.axis_index("grp")
        if far:
            group = pairing[group]
        copies = []
        for n, source in enumerate(sources(lax.axis_index("blk"))):
            first = pl.multiple_of(ownership[group, source] * height, height)
            copies.append(pltpu.make_async_copy(blocks[n], y_ref.at[pl.ds(first, height)], sems.at[n]))
            copies[n].start()
        for copy in copies:
            copy.wait()
        for k in range(0, depth, 256):
            yt_ref[k : k + 256, :] = y_ref[:, k : k + 256].T

    for r in range(ROWS):
        for w in range(windows):
            real = slice(w * freqs, (w + 1) * freqs)
            imag = slice((windows + w) * freqs, (windows + w + 1) * freqs)
            x_real, x_imag = x_ref[r : r + 1, real], x_ref[r : r + 1, imag]
            t_real, t_imag = twiddle_ref[0], twiddle_ref[1]
            left_ref[r * lags : (r + 1) * lags, real] = x_real * t_real + x_imag * t_imag
            left_ref[r * lags : (r + 1) * lags, imag] = x_imag * t_real - x_real * t_imag
    result = jnp.dot(left_ref[...], yt_ref[...], preferred_element_type=jnp.float32)
    scale = np.float32(1.0 / (windows * np.sqrt(freqs)))
    for r in range(ROWS):
        out_ref[r] = (result[r * lags : (r + 1) * lags] * scale).T.astype(out_ref.dtype)


def correlate(far, ownership, pairing, x, twiddle, blocks):
    rows, depth = x.shape
    lags = twiddle.shape[1]
    columns = rows * 8
    return pl.pallas_call(
        functools.partial(correlate_kernel, far),
        grid_spec=pltpu.PrefetchScalarGridSpec(
            num_scalar_prefetch=2,
            grid=(rows // ROWS,),
            in_specs=[
                pl.BlockSpec((ROWS, depth), lambda i, *_: (i, 0)),
                pl.BlockSpec(twiddle.shape, lambda i, *_: (0, 0, 0)),
            ]
            + [pl.BlockSpec(memory_space=pl.ANY)] * 8,
            out_specs=pl.BlockSpec((ROWS, columns, lags), lambda i, *_: (i, 0, 0)),
            scratch_shapes=[
                pltpu.VMEM((columns, depth), jnp.bfloat16),
                pltpu.VMEM((depth, columns), jnp.bfloat16),
                pltpu.VMEM((ROWS * lags, depth), jnp.bfloat16),
                pltpu.SemaphoreType.DMA((8,)),
            ],
        ),
        out_shape=jax.ShapeDtypeStruct((rows, columns, lags), jnp.bfloat16),
        compiler_params=pltpu.CompilerParams(vmem_limit_bytes=48 * 2**20),
        cost_estimate=pl.CostEstimate(
            flops=2 * rows * lags * depth * columns, bytes_accessed=2**22, transcendentals=0
        ),
    )(ownership, pairing, x, twiddle, *blocks)


def shards(spectra, ownership, pairing):
    rows, parts, windows, freqs = spectra.shape
    twiddle = jnp.asarray(twiddle_table(freqs, LAGS))
    own = spectra.reshape(rows, parts * windows * freqs)
    partner = exchange(own, pairing[0])
    near = correlate(False, ownership, pairing, own, twiddle, gather(own))
    far = correlate(True, ownership, pairing, own, twiddle, gather(partner))
    return near, far


def solution(mesh):
    in_specs = (P(("grp", "blk"), None, None, None), P(), P())
    out_specs = (P(("grp", "blk"), None, None), P(("grp", "blk"), None, None))
    return jax.shard_map(shards, mesh=mesh, in_specs=in_specs, out_specs=out_specs, check_vma=False)
```

```python
import functools

import jax
import jax.numpy as jnp
import ml_dtypes
import numpy as np
from jax import lax
from jax.experimental import pallas as pl
from jax.experimental.pallas import tpu as pltpu
from jax.sharding import PartitionSpec as P

LAGS = 128
ROWS = 8


def twiddle_table(freq_count, lag_count):
    freqs = np.arange(freq_count)[None, :]
    shifts = np.arange(lag_count)[:, None] - lag_count // 2
    angle = np.pi * ((freqs * shifts) % (2 * freq_count)) / freq_count
    return np.stack([np.cos(angle), -np.sin(angle)]).astype(ml_dtypes.bfloat16)


def sources(place):
    column, y = place // 4 * 4, place % 4
    up, down, over = (y + 1) % 4, (y + 3) % 4, (y + 2) % 4
    other = 4 - column
    return (
        column + y, other + y, column + down, column + up,
        column + over, other + down, other + up, other + over,
    )


def send(block, step):
    return lax.ppermute(block, "blk", [(i, step(i)) for i in range(8)])


def across(block):
    return send(block, lambda i: i ^ 4)


def upward(block):
    return send(block, lambda i: i & 4 | (i + 1) & 3)


def downward(block):
    return send(block, lambda i: i & 4 | (i - 1) & 3)


def over(block):
    return send(block, lambda i: i & 4 | (i + 2) & 3)


def to_group(block, mask):
    return lax.ppermute(block, "grp", [(i, i ^ mask) for i in range(lax.axis_size("grp"))])


def exchange(block, mask):
    swapped = jnp.where(mask & 1 == 1, to_group(block, 1), block)
    branches = [lambda v: v] + [
        functools.partial(to_group, mask=m) for m in range(2, lax.axis_size("grp"), 2)
    ]
    return lax.switch(mask >> 1, branches, swapped)


def correlate_kernel(far, ownership, pairing, x_ref, twiddle_ref, *refs):
    blocks, (out_ref, y_ref, turned_ref, sems) = refs[:8], refs[-4:]
    step = pl.program_id(0)
    depth = y_ref.shape[1]
    lags, freqs = twiddle_ref.shape[1:]
    windows = depth // freqs // 2
    height = y_ref.shape[0] // 8

    def fill():
        for r in range(ROWS):
            for w in range(windows):
                real = slice(w * freqs, (w + 1) * freqs)
                imag = slice((windows + w) * freqs, (windows + w + 1) * freqs)
                x_real, x_imag = x_ref[r : r + 1, real], x_ref[r : r + 1, imag]
                t_real, t_imag = twiddle_ref[0], twiddle_ref[1]
                turned_ref[r * lags : (r + 1) * lags, real] = x_real * t_real + x_imag * t_imag
                turned_ref[r * lags : (r + 1) * lags, imag] = x_imag * t_real - x_real * t_imag

    @pl.when(step == 0)
    def _():
        group = lax.axis_index("grp")
        if far:
            group = pairing[group]
        copies = []
        for n, source in enumerate(sources(lax.axis_index("blk"))):
            first = pl.multiple_of(ownership[group, source] * height, height)
            copies.append(pltpu.make_async_copy(blocks[n], y_ref.at[pl.ds(first, height)], sems.at[n]))
            copies[n].start()
        for copy in copies:
            copy.wait()

    fill()
    result = lax.dot_general(
        y_ref[...], turned_ref[...], (((1,), (1,)), ((), ())), preferred_element_type=jnp.float32
    )
    scale = np.float32(1.0 / (windows * np.sqrt(freqs)))
    for r in range(ROWS):
        out_ref[r] = (result[:, r * lags : (r + 1) * lags] * scale).astype(out_ref.dtype)


def correlate(far, ownership, pairing, x, twiddle, blocks, steps=None, out=None):
    rows, depth = x.shape
    lags = twiddle.shape[1]
    columns = rows * 8
    first_step, last_step = steps or (0, rows // ROWS)
    extra = [] if out is None else [out]
    return pl.pallas_call(
        functools.partial(correlate_kernel, far),
        grid_spec=pltpu.PrefetchScalarGridSpec(
            num_scalar_prefetch=2,
            grid=(last_step - first_step,),
            in_specs=[
                pl.BlockSpec((ROWS, depth), lambda i, *_: (first_step + i, 0)),
                pl.BlockSpec(twiddle.shape, lambda i, *_: (0, 0, 0)),
            ]
            + [pl.BlockSpec(memory_space=pl.ANY)] * (8 + len(extra)),
            out_specs=pl.BlockSpec((ROWS, columns, lags), lambda i, *_: (first_step + i, 0, 0)),
            scratch_shapes=[
                pltpu.VMEM((columns, depth), jnp.bfloat16),
                pltpu.VMEM((ROWS * lags, depth), jnp.bfloat16),
                pltpu.SemaphoreType.DMA((8,)),
            ],
        ),
        out_shape=jax.ShapeDtypeStruct((rows, columns, lags), jnp.bfloat16),
        input_output_aliases={12: 0} if extra else {},
        compiler_params=pltpu.CompilerParams(vmem_limit_bytes=40 * 2**20),
        cost_estimate=pl.CostEstimate(
            flops=2 * (last_step - first_step) * ROWS * lags * depth * columns,
            bytes_accessed=2**22,
            transcendentals=0,
        ),
    )(ownership, pairing, x, twiddle, *blocks, *extra)


def shards(spectra, ownership, pairing):
    rows, parts, windows, freqs = spectra.shape
    twiddle = jnp.asarray(twiddle_table(freqs, LAGS))
    own = spectra.reshape(rows, parts * windows * freqs)
    beside, below, above, opposite = across(own), upward(own), downward(own), over(own)
    partner = exchange(own, pairing[0])
    beside, below, above, opposite, partner = lax.optimization_barrier(
        (beside, below, above, opposite, partner)
    )
    far_beside, far_below, far_above = across(partner), upward(partner), downward(partner)
    near_blocks = [
        own, beside, below, above, opposite,
        upward(beside), downward(beside), across(opposite),
    ]
    halves = rows // ROWS // 2
    near = correlate(False, ownership, pairing, own, twiddle, near_blocks, (0, halves))
    far_opposite = downward(far_above)
    far_beside_above = across(far_above)
    far_beside_below = upward(far_beside)
    far_opposite, far_beside_above, far_beside_below, near = lax.optimization_barrier(
        (far_opposite, far_beside_above, far_beside_below, near)
    )
    far_beside_opposite = across(far_opposite)
    near = correlate(False, ownership, pairing, own, twiddle, near_blocks, (halves, 2 * halves), near)
    far = correlate(
        True, ownership, pairing, own, twiddle,
        [partner, far_beside, far_below, far_above, far_opposite,
         far_beside_below, far_beside_above, far_beside_opposite],
    )
    return near, far


def solution(mesh):
    in_specs = (P(("grp", "blk"), None, None, None), P(), P())
    out_specs = (P(("grp", "blk"), None, None), P(("grp", "blk"), None, None))
    return jax.shard_map(shards, mesh=mesh, in_specs=in_specs, out_specs=out_specs, check_vma=False)
```

```python
import functools

import jax
import jax.numpy as jnp
import ml_dtypes
import numpy as np
from jax import lax
from jax.experimental import pallas as pl
from jax.experimental.pallas import tpu as pltpu
from jax.sharding import PartitionSpec as P

LAGS = 128
ROWS = 8


def twiddle_table(freq_count, lag_count):
    freqs = np.arange(freq_count)[None, :]
    shifts = np.arange(lag_count)[:, None] - lag_count // 2
    angle = np.pi * ((freqs * shifts) % (2 * freq_count)) / freq_count
    return np.stack([np.cos(angle), -np.sin(angle)]).astype(ml_dtypes.bfloat16)


def sources(place):
    column, y = place // 4 * 4, place % 4
    up, down, over = (y + 1) % 4, (y + 3) % 4, (y + 2) % 4
    other = 4 - column
    return (
        column + y, other + y, column + down, column + up,
        column + over, other + down, other + up, other + over,
    )


def send(block, step):
    return lax.ppermute(block, "blk", [(i, step(i)) for i in range(8)])


def across(block):
    return send(block, lambda i: i ^ 4)


def upward(block):
    return send(block, lambda i: i & 4 | (i + 1) & 3)


def downward(block):
    return send(block, lambda i: i & 4 | (i - 1) & 3)


def across_downward(block):
    return send(block, lambda i: (i ^ 4) & 4 | (i - 1) & 3)


def over(block):
    return send(block, lambda i: i & 4 | (i + 2) & 3)


def to_group(block, mask):
    return lax.ppermute(block, "grp", [(i, i ^ mask) for i in range(lax.axis_size("grp"))])


def exchange(block, mask):
    swapped = jnp.where(mask & 1 == 1, to_group(block, 1), block)
    branches = [lambda v: v] + [
        functools.partial(to_group, mask=m) for m in range(2, lax.axis_size("grp"), 2)
    ]
    return lax.switch(mask >> 1, branches, swapped)


def correlate_kernel(far, ownership, pairing, x_ref, twiddle_ref, *refs):
    blocks, (out_ref, y_ref, turned_ref, sems) = refs[:8], refs[-4:]
    step = pl.program_id(0)
    depth = y_ref.shape[1]
    lags, freqs = twiddle_ref.shape[1:]
    windows = depth // freqs // 2
    height = y_ref.shape[0] // 8

    def fill():
        for r in range(ROWS):
            for w in range(windows):
                real = slice(w * freqs, (w + 1) * freqs)
                imag = slice((windows + w) * freqs, (windows + w + 1) * freqs)
                x_real, x_imag = x_ref[r : r + 1, real], x_ref[r : r + 1, imag]
                t_real, t_imag = twiddle_ref[0], twiddle_ref[1]
                turned_ref[r * lags : (r + 1) * lags, real] = x_real * t_real + x_imag * t_imag
                turned_ref[r * lags : (r + 1) * lags, imag] = x_imag * t_real - x_real * t_imag

    @pl.when(step == 0)
    def _():
        group = lax.axis_index("grp")
        if far:
            group = pairing[group]
        copies = []
        for n, source in enumerate(sources(lax.axis_index("blk"))):
            first = pl.multiple_of(ownership[group, source] * height, height)
            copies.append(pltpu.make_async_copy(blocks[n], y_ref.at[pl.ds(first, height)], sems.at[n]))
            copies[n].start()
        for copy in copies:
            copy.wait()

    fill()
    result = lax.dot_general(
        y_ref[...], turned_ref[...], (((1,), (1,)), ((), ())), preferred_element_type=jnp.float32
    )
    scale = np.float32(1.0 / (windows * np.sqrt(freqs)))
    for r in range(ROWS):
        out_ref[r] = (result[:, r * lags : (r + 1) * lags] * scale).astype(out_ref.dtype)


def correlate(far, ownership, pairing, x, twiddle, blocks):
    rows, depth = x.shape
    lags = twiddle.shape[1]
    columns = rows * 8
    return pl.pallas_call(
        functools.partial(correlate_kernel, far),
        grid_spec=pltpu.PrefetchScalarGridSpec(
            num_scalar_prefetch=2,
            grid=(rows // ROWS,),
            in_specs=[
                pl.BlockSpec((ROWS, depth), lambda i, *_: (i, 0)),
                pl.BlockSpec(twiddle.shape, lambda i, *_: (0, 0, 0)),
            ]
            + [pl.BlockSpec(memory_space=pl.ANY)] * 8,
            out_specs=pl.BlockSpec((ROWS, columns, lags), lambda i, *_: (i, 0, 0)),
            scratch_shapes=[
                pltpu.VMEM((columns, depth), jnp.bfloat16),
                pltpu.VMEM((ROWS * lags, depth), jnp.bfloat16),
                pltpu.SemaphoreType.DMA((8,)),
            ],
        ),
        out_shape=jax.ShapeDtypeStruct((rows, columns, lags), jnp.bfloat16),
        compiler_params=pltpu.CompilerParams(vmem_limit_bytes=40 * 2**20),
        cost_estimate=pl.CostEstimate(
            flops=2 * rows * lags * depth * columns,
            bytes_accessed=2**22,
            transcendentals=0,
        ),
    )(ownership, pairing, x, twiddle, *blocks)


def shards(spectra, ownership, pairing):
    rows, parts, windows, freqs = spectra.shape
    twiddle = jnp.asarray(twiddle_table(freqs, LAGS))
    own = spectra.reshape(rows, parts * windows * freqs)
    beside, below, above, opposite = across(own), upward(own), downward(own), over(own)
    partner = exchange(own, pairing[0])
    beside, below, above, opposite, partner = lax.optimization_barrier(
        (beside, below, above, opposite, partner)
    )
    far_beside, far_below, far_above = across(partner), upward(partner), downward(partner)
    near_blocks = [
        own, beside, below, above, opposite,
        upward(beside), downward(beside), across(opposite),
    ]
    near = correlate(False, ownership, pairing, own, twiddle, near_blocks)
    far = correlate(
        True, ownership, pairing, own, twiddle,
        [partner, far_beside, far_below, far_above, downward(far_above),
         upward(far_beside), across(far_above), across_downward(far_above)],
    )
    return near, far


def solution(mesh):
    in_specs = (P(("grp", "blk"), None, None, None), P(), P())
    out_specs = (P(("grp", "blk"), None, None), P(("grp", "blk"), None, None))
    return jax.shard_map(shards, mesh=mesh, in_specs=in_specs, out_specs=out_specs, check_vma=False)
```

```python
import functools

import jax
import jax.numpy as jnp
import ml_dtypes
import numpy as np
from jax import lax
from jax.experimental import pallas as pl
from jax.experimental.pallas import tpu as pltpu
from jax.sharding import PartitionSpec as P

LAGS = 128
ROWS = 16


def twiddle_table(freq_count, lag_count):
    freqs = np.arange(freq_count)[None, :]
    shifts = np.arange(lag_count)[:, None] - lag_count // 2
    angle = np.pi * ((freqs * shifts) % (2 * freq_count)) / freq_count
    return np.stack([np.cos(angle), -np.sin(angle)]).astype(ml_dtypes.bfloat16)


def sources(place):
    column, y = place // 4 * 4, place % 4
    up, down, over = (y + 1) % 4, (y + 3) % 4, (y + 2) % 4
    other = 4 - column
    return (
        column + y, other + y, column + down, column + up,
        column + over, other + down, other + up, other + over,
    )


def send(block, step):
    return lax.ppermute(block, "blk", [(i, step(i)) for i in range(8)])


def across(block):
    return send(block, lambda i: i ^ 4)


def upward(block):
    return send(block, lambda i: i & 4 | (i + 1) & 3)


def downward(block):
    return send(block, lambda i: i & 4 | (i - 1) & 3)


def across_downward(block):
    return send(block, lambda i: (i ^ 4) & 4 | (i - 1) & 3)


def over(block):
    return send(block, lambda i: i & 4 | (i + 2) & 3)


def to_group(block, mask):
    return lax.ppermute(block, "grp", [(i, i ^ mask) for i in range(lax.axis_size("grp"))])


def exchange(block, mask):
    swapped = jnp.where(mask & 1 == 1, to_group(block, 1), block)
    branches = [lambda v: v] + [
        functools.partial(to_group, mask=m) for m in range(2, lax.axis_size("grp"), 2)
    ]
    return lax.switch(mask >> 1, branches, swapped)


def correlate_kernel(far, ownership, pairing, x_ref, twiddle_ref, *refs):
    blocks, (out_ref, y_ref, turned_ref, sems) = refs[:8], refs[-4:]
    step = pl.program_id(0)
    depth = y_ref.shape[1]
    lags, freqs = twiddle_ref.shape[1:]
    windows = depth // freqs // 2
    height = y_ref.shape[0] // 8

    def fill():
        for r in range(ROWS):
            for w in range(windows):
                real = slice(w * freqs, (w + 1) * freqs)
                imag = slice((windows + w) * freqs, (windows + w + 1) * freqs)
                x_real, x_imag = x_ref[r : r + 1, real], x_ref[r : r + 1, imag]
                t_real, t_imag = twiddle_ref[0], twiddle_ref[1]
                turned_ref[r * lags : (r + 1) * lags, real] = x_real * t_real + x_imag * t_imag
                turned_ref[r * lags : (r + 1) * lags, imag] = x_imag * t_real - x_real * t_imag

    @pl.when(step == 0)
    def _():
        group = lax.axis_index("grp")
        if far:
            group = pairing[group]
        copies = []
        for n, source in enumerate(sources(lax.axis_index("blk"))):
            first = pl.multiple_of(ownership[group, source] * height, height)
            copies.append(pltpu.make_async_copy(blocks[n], y_ref.at[pl.ds(first, height)], sems.at[n]))
            copies[n].start()
        for copy in copies:
            copy.wait()

    fill()
    result = lax.dot_general(
        y_ref[...], turned_ref[...], (((1,), (1,)), ((), ())), preferred_element_type=jnp.float32
    )
    scale = np.float32(1.0 / (windows * np.sqrt(freqs)))
    for r in range(ROWS):
        out_ref[r] = (result[:, r * lags : (r + 1) * lags] * scale).astype(out_ref.dtype)


def correlate(far, ownership, pairing, x, twiddle, blocks):
    rows, depth = x.shape
    lags = twiddle.shape[1]
    columns = rows * 8
    return pl.pallas_call(
        functools.partial(correlate_kernel, far),
        grid_spec=pltpu.PrefetchScalarGridSpec(
            num_scalar_prefetch=2,
            grid=(rows // ROWS,),
            in_specs=[
                pl.BlockSpec((ROWS, depth), lambda i, *_: (i, 0)),
                pl.BlockSpec(twiddle.shape, lambda i, *_: (0, 0, 0)),
            ]
            + [pl.BlockSpec(memory_space=pl.ANY)] * 8,
            out_specs=pl.BlockSpec((ROWS, columns, lags), lambda i, *_: (i, 0, 0)),
            scratch_shapes=[
                pltpu.VMEM((columns, depth), jnp.bfloat16),
                pltpu.VMEM((ROWS * lags, depth), jnp.bfloat16),
                pltpu.SemaphoreType.DMA((8,)),
            ],
        ),
        out_shape=jax.ShapeDtypeStruct((rows, columns, lags), jnp.bfloat16),
        compiler_params=pltpu.CompilerParams(vmem_limit_bytes=40 * 2**20),
        cost_estimate=pl.CostEstimate(
            flops=2 * rows * lags * depth * columns,
            bytes_accessed=2**22,
            transcendentals=0,
        ),
    )(ownership, pairing, x, twiddle, *blocks)


def shards(spectra, ownership, pairing):
    rows, parts, windows, freqs = spectra.shape
    twiddle = jnp.asarray(twiddle_table(freqs, LAGS))
    own = spectra.reshape(rows, parts * windows * freqs)
    beside, below, above, opposite = across(own), upward(own), downward(own), over(own)
    partner = exchange(own, pairing[0])
    beside, below, above, opposite, partner = lax.optimization_barrier(
        (beside, below, above, opposite, partner)
    )
    far_beside, far_below, far_above = across(partner), upward(partner), downward(partner)
    near_blocks = [
        own, beside, below, above, opposite,
        upward(beside), downward(beside), across(opposite),
    ]
    near = correlate(False, ownership, pairing, own, twiddle, near_blocks)
    far = correlate(
        True, ownership, pairing, own, twiddle,
        [partner, far_beside, far_below, far_above, downward(far_above),
         upward(far_beside), across(far_above), across_downward(far_above)],
    )
    return near, far


def solution(mesh):
    in_specs = (P(("grp", "blk"), None, None, None), P(), P())
    out_specs = (P(("grp", "blk"), None, None), P(("grp", "blk"), None, None))
    return jax.shard_map(shards, mesh=mesh, in_specs=in_specs, out_specs=out_specs, check_vma=False)
```
